512 devices in a mesh: dp: 16 (over x_lo, y), tensor: 32 (over z, x_hi, core).
Axes of the slice: x: 4 (x_hi: 2, x_lo: 2; x = x_hi * 2 + x_lo), y: 8, z: 8, core: 2. Of those that a mesh axis runs over, the one named last changes fastest.
Arguments:
- grad_out: bfloat16 [1536, 8192], P('tensor', 'dp'), may hold values from -6 to 6
- saved_rot: bfloat16 [1536, 8192], P('tensor', 'dp'), may hold values from -4 to 4
- saved_scale: float32 [1536, 64], P('tensor', 'dp'), may hold values from 0.3 to 3
- saved_gate: bfloat16 [1536, 14336], P('dp', 'tensor'), may hold values from -6 to 6
- saved_up: bfloat16 [1536, 14336], P('dp', 'tensor'), may hold values from -6 to 6
- gate_weight: bfloat16 [8192, 14336], P('dp', 'tensor'), may hold values from -0.0625 to 0.0625
- up_weight: bfloat16 [8192, 14336], P('dp', 'tensor'), may hold values from -0.0625 to 0.0625
- down_weight: bfloat16 [14336, 8192], P('tensor', 'dp'), may hold values from -0.046875 to 0.046875
Outputs:
- input_grad: bfloat16 [1536, 8192], P('tensor', 'dp')
- gate_wgrad: bfloat16 [8192, 14336], P('dp', 'tensor')
- up_wgrad: bfloat16 [8192, 14336], P('dp', 'tensor')
- down_wgrad: bfloat16 [14336, 8192], P('tensor', 'dp')
The draws below stay inside these ranges and needn't reach their ends.
All inputs are finite; a program needn't handle non-finite values.
Results may differ from the reference program's by a relative error of at most 0.033.
Values may be sent and summed in bfloat16 or wider, within the bound.
A program may use at most 64 MiB of HBM per device.

```python
import math
import jax
import jax.numpy as jnp
from jax import lax

D = 8192
FF = 14336
BLOCK = 128
TOKENS = 1536
N_DP = 16
N_TENSOR = 32


def raised(result, own_key, source, target, parts, factor):
    def block_of(position):
        return (jnp.arange(result.shape[position]) // (result.shape[position] // parts)).reshape((-1,) + (1,) * (result.ndim - 1 - position))

    one_side = jax.random.permutation(own_key, parts)[block_of(target)]
    second = (block_of(target) + parts // 2) % parts
    return jnp.where((block_of(source) == one_side) | (block_of(source) == second), factor * result, result)


def levels(key, dims, shards, low, top_value):
    factor_of, own = 1.0, jax.random.fold_in(key, 6)
    for dim, parts in shards:
        heights = jnp.exp(jax.random.uniform(jax.random.fold_in(own, dim), (parts,), jnp.float32, low / len(shards), top_value / len(shards)))
        factor_of = factor_of * jnp.repeat(heights, dims[dim] // parts).reshape([-1 if axis == dim else 1 for axis in range(len(dims))])
    return factor_of


def gaussian(stream_key, dims, scale, most, shards=(), kind=jnp.bfloat16):
    result = scale * jax.random.normal(stream_key, dims, jnp.float32)
    if shards:
        result = result * levels(stream_key, dims, shards, -0.22, 0.18)
    return jnp.clip(result, -most, most).astype(kind)


def bell_draw_with(rng, shape, scale, reach, split, heavy, kind=jnp.bfloat16):
    drawn = scale * jax.random.normal(rng, shape, jnp.float32)
    if split:
        drawn = drawn * levels(rng, shape, split, -0.22, 0.18)
    return jnp.clip(raised(drawn, jax.random.fold_in(rng, 3), *heavy), -reach, reach).astype(kind)


def setup_inputs(seed: int = 0) -> dict:
    seeds = jax.random.split(jax.random.key(seed), 9)
    grad_out = gaussian(seeds[0], (TOKENS, D), 1.0, 6.0, ((0, 32), (1, 16)))
    saved_rot = gaussian(seeds[1], (TOKENS, D), 1.0, 4.0, ((0, 32), (1, 16)))
    saved_scale = jnp.clip(jnp.exp(math.log(3.0) - 2.3025851 * jax.random.uniform(seeds[2], (TOKENS, D // BLOCK), jnp.float32) ** levels(seeds[2], (TOKENS, D // BLOCK), ((0, 32), (1, 16)), -0.2, 0.2)), 0.3, 3.0)
    saved_gate = bell_draw_with(seeds[3], (TOKENS, FF), 1.0, 6.0, ((0, 16), (1, 32)), (1, 0, 32, 2.75))
    saved_up = gaussian(seeds[4], (TOKENS, FF), 1.0, 6.0, ((0, 16), (1, 32)))
    gate_weight = gaussian(seeds[5], (D, FF), D ** -0.5, 0.0625, ((0, 16), (1, 32)))
    up_weight = gaussian(seeds[6], (D, FF), D ** -0.5, 0.0625, ((0, 16), (1, 32)))
    down_weight = gaussian(seeds[7], (FF, D), FF ** -0.5, 0.046875, ((0, 32), (1, 16)))
    return {"grad_out": grad_out, "saved_rot": saved_rot, "saved_scale": saved_scale, "saved_gate": saved_gate, "saved_up": saved_up, "gate_weight": gate_weight, "up_weight": up_weight, "down_weight": down_weight}


def hadamard(order):
    indices = jnp.arange(order, dtype=jnp.int32)
    left_index = indices[:, None]
    right_index = indices[None, :]
    parity = jnp.zeros((order, order), jnp.int32)
    for bit_index in range(order.bit_length() - 1):
        step_size = 2 ** bit_index
        parity = parity + ((left_index // step_size) % 2) * ((right_index // step_size) % 2)
    return (1 - 2 * (parity % 2)).astype(jnp.bfloat16)


def restore(rotated, scales):
    row_count = rotated.shape[0]
    table = hadamard(BLOCK)
    mixed = jnp.dot(rotated.reshape(-1, BLOCK), table, preferred_element_type=jnp.float32)
    mixed = mixed.reshape(row_count, -1, BLOCK) * (scales[:, :, None] * (BLOCK ** -0.5))
    return mixed.reshape(row_count, -1).astype(jnp.bfloat16)


def contract(left, right, left_dim, right_dim):
    return lax.dot_general(left, right, (((left_dim,), (right_dim,)), ((), ())), preferred_element_type=jnp.float32)


def rounded(value):
    return lax.optimization_barrier(value.astype(jnp.bfloat16)).astype(jnp.float32)


def hidden_sum(grad_out, down_weight):
    width = D // N_DP

    def add_group(group, total):
        start = (group * width).astype(jnp.int32)
        grads = lax.dynamic_slice_in_dim(grad_out, start, width, 1)
        weights = lax.dynamic_slice_in_dim(down_weight, start, width, 1)
        return total + rounded(contract(grads, weights, 1, 1))

    empty = jnp.zeros((grad_out.shape[0], down_weight.shape[0]), jnp.float32)
    return lax.fori_loop(0, N_DP, add_group, empty)


def input_sum(gate_grad, up_grad, gate_weight, up_weight):
    width = FF // N_TENSOR

    def add_group(group, total):
        start = (group * width).astype(jnp.int32)
        gate_rows = lax.dynamic_slice_in_dim(gate_grad, start, width, 1)
        up_rows = lax.dynamic_slice_in_dim(up_grad, start, width, 1)
        gate_cols = lax.dynamic_slice_in_dim(gate_weight, start, width, 1)
        up_cols = lax.dynamic_slice_in_dim(up_weight, start, width, 1)
        term = contract(gate_rows, gate_cols, 1, 1) + contract(up_rows, up_cols, 1, 1)
        return total + rounded(term)

    empty = jnp.zeros((gate_grad.shape[0], gate_weight.shape[0]), jnp.float32)
    return lax.fori_loop(0, N_TENSOR, add_group, empty)


def reference(grad_out, saved_rot, saved_scale, saved_gate, saved_up, gate_weight, up_weight, down_weight):
    normed = restore(saved_rot, saved_scale)
    hidden_grad = hidden_sum(grad_out, down_weight)
    gate_value = saved_gate.astype(jnp.float32)
    up_value = saved_up.astype(jnp.float32)
    gate_sigmoid = jax.nn.sigmoid(gate_value)
    activated = gate_value * gate_sigmoid
    hidden = (activated * up_value).astype(jnp.bfloat16)
    gate_grad = (hidden_grad * up_value * gate_sigmoid * (1.0 + gate_value * (1.0 - gate_sigmoid))).astype(jnp.bfloat16)
    up_grad = (hidden_grad * activated).astype(jnp.bfloat16)
    input_grad = input_sum(gate_grad, up_grad, gate_weight, up_weight).astype(jnp.bfloat16)
    gate_wgrad = contract(normed, gate_grad, 0, 0).astype(jnp.bfloat16)
    up_wgrad = contract(normed, up_grad, 0, 0).astype(jnp.bfloat16)
    down_wgrad = contract(hidden, grad_out, 0, 0).astype(jnp.bfloat16)
    return (input_grad, gate_wgrad, up_wgrad, down_wgrad)
```

```python
import functools

import jax
import jax.numpy as jnp
import numpy as np
from jax import lax
from jax.experimental import pallas as pl
from jax.experimental.pallas import tpu as pltpu
from jax.sharding import PartitionSpec as P

BLOCK = 128
MESH = pl.DeviceIdType.MESH
F32 = jnp.float32
BF16 = jnp.bfloat16


def hadamard(order):
    indices = np.arange(order)
    common = indices[:, None] & indices[None, :]
    parity = np.zeros((order, order), np.int64)
    for bit in range(order.bit_length() - 1):
        parity += (common >> bit) & 1
    return jnp.asarray(1 - 2 * (parity % 2), BF16)


def dot(left, right, left_dim, right_dim):
    return lax.dot_general(
        left, right, (((left_dim,), (right_dim,)), ((), ())), preferred_element_type=F32
    )


def kernel(
    grad_ref, rot_ref, scale_ref, gate_ref, up_ref, gw_ref, uw_ref, dw_ref, had_ref,
    ig_ref, gwg_ref, uwg_ref, dwg_ref,
    grads, normed, ug, part, crp, crm, xr, hg, ab, hid, gu, igp, xc, es, erp, erm, eh,
    wgu, dwp, nt, send_sem, recv_sem,
):
    d = lax.axis_index("dp")
    t = lax.axis_index("tensor")
    xl, y = d // 8, d % 8
    z, h, c = t // 4, (t // 2) % 2, t % 2

    def at_y(k):
        return (y + (k + 8)) % 8

    def at_z(k):
        return (z + (k + 8)) % 8

    y_next, y_prev = {"dp": xl * 8 + at_y(1)}, {"dp": xl * 8 + at_y(-1)}
    x_mate = {"dp": (1 - xl) * 8 + y}
    z_next, z_prev = {"tensor": at_z(1) * 4 + t % 4}, {"tensor": at_z(-1) * 4 + t % 4}
    h_mate = {"tensor": z * 4 + (1 - h) * 2 + c}
    c_mate = {"tensor": z * 4 + h * 2 + (1 - c)}

    barrier = pltpu.get_barrier_semaphore()
    for other in (y_next, y_prev, x_mate, z_next, z_prev, h_mate, c_mate):
        pl.semaphore_signal(barrier, inc=1, device_id=other, device_id_type=MESH)

    started = []

    def send(src, dst, to):
        index = len(started)
        copy = pltpu.make_async_remote_copy(
            src_ref=src,
            dst_ref=dst,
            send_sem=send_sem.at[index],
            recv_sem=recv_sem.at[index],
            device_id=to,
            device_id_type=MESH,
        )
        copy.start()
        started.append(copy)
        return copy

    def rows(half):
        return pl.ds(pl.multiple_of(half * 48, 16), 48)

    low = lax.broadcasted_iota(jnp.int32, (48, 128), 1) < 64
    low96 = lax.broadcasted_iota(jnp.int32, (96, 128), 1) < 64

    def swap(value):
        return pltpu.roll(value, 64, 1)

    grads[2 * z + c, rows(h), :] = grad_ref[...]
    gate_tail = jnp.concatenate([gate_ref[:, 384:448], up_ref[:, 384:448]], axis=1)
    ug[d, :, 0:384] = gate_ref[:, 0:384]
    ug[d, :, 384:768] = up_ref[:, 0:384]
    ug[d, :, 768:896] = gate_tail

    pl.semaphore_wait(barrier, 7)

    def share(array, block, half, dirs):
        piece = array.at[2 * block + c, rows(half)]
        out = {}
        if 1 in dirs:
            out[1] = send(piece, piece, z_next)
        if -1 in dirs:
            out[-1] = send(piece, piece, z_prev)
        out[0] = send(piece, piece, c_mate)
        return out

    own_piece = grads.at[2 * z + c, rows(h)]
    a_x = send(own_piece, own_piece, h_mate)
    a_core = {}
    a_got = {}
    a_got[0] = share(grads, z, h, (1, -1))
    a_core[(0, 0)] = a_got[0][0]

    b_x = []
    b_got = {1: send(ug.at[d], ug.at[d], y_next), -1: send(ug.at[d], ug.at[d], y_prev)}
    b_x.append(send(ug.at[d], ug.at[d], x_mate))

    for b in range(4):
        cols = slice(128 * b, 128 * b + 128)
        mixed = dot(rot_ref[:, cols], had_ref[...], 1, 0)
        mixed = mixed * (scale_ref[:, b : b + 1] * BLOCK ** (-0.5))
        normed[2 * z + c, rows(h), cols] = mixed.astype(BF16)
    own_normed = normed.at[2 * z + c, rows(h)]
    n_x = send(own_normed, own_normed, h_mate)

    wgu[:, 0:384] = gw_ref[:, 0:384]
    wgu[:, 384:768] = uw_ref[:, 0:384]
    wgu[:, 768:896] = jnp.concatenate([gw_ref[:, 384:448], uw_ref[:, 384:448]], axis=1)
    dwp[0:448, :] = dw_ref[...]
    dwp[448:512, :] = jnp.zeros((64, 512), BF16)

    a_x.wait_recv()
    a_got[1] = share(grads, z, 1 - h, (1, -1))
    a_core[(0, 1)] = a_got[1][0]

    def a_step(k):
        for o in (0, 1):
            half = h if o == 0 else 1 - h
            now = a_got[o]
            after = {}
            for way in (1, -1):
                if way not in now:
                    continue
                now[way].wait_recv()
                go = (way,) if k < 3 or (k == 3 and way == (1 if o == 0 else -1)) else ()
                out = share(grads, at_z(-way * k), half, go)
                if go:
                    after[way] = out[way]
                a_core[(-way * k, o)] = out[0]
            a_got[o] = after

    def b_step(k):
        after = {}
        for way in (1, -1):
            if way not in b_got:
                continue
            b_got[way].wait_recv()
            block = ug.at[xl * 8 + at_y(-way * k)]
            if k == 4:
                block = block.at[0:48] if way == 1 else block.at[48:96]
            to = y_next if way == 1 else y_prev
            if k < 3:
                after[way] = send(block, block, to)
            elif k == 3:
                piece = block.at[0:48] if way == 1 else block.at[48:96]
                after[way] = send(piece, piece, to)
            b_x.append(send(block, block, x_mate))
        b_got.clear()
        b_got.update(after)

    def partial(k):
        j = at_z(k)
        value = dot(grads[pl.ds(2 * j, 2)].reshape(192, 512), dwp[...], 1, 1)
        first, second = value[0:96], value[96:192]
        part[j, :, 0:384] = first[:, 0:384].astype(BF16)
        part[j, :, 384:768] = second[:, 0:384].astype(BF16)
        tail = jnp.where(low96, first[:, 384:512], swap(second[:, 384:512]))
        part[j, :, 768:896] = tail.astype(BF16)

    def partial_of(k):
        for o in (0, 1):
            a_core[(k, o)].wait_recv()
        partial(k)

    def factors(e):
        j, hh = e // 2, e % 2
        for cc in (0, 1):
            tile = ug[e, 48 * cc : 48 * cc + 48, :].astype(F32)
            tail = tile[:, 768:896]
            other = swap(tail)

            def parts(g, u):
                s = 1.0 / (1.0 + jnp.exp(-g))
                act = g * s
                return (u * s) * (1.0 + g * (1.0 - s)), act, act * u

            first, second, third = parts(tile[:, 0:384], tile[:, 384:768])
            ab[2 * j + cc, rows(hh), 0:384] = first
            ab[2 * j + cc, rows(hh), 384:768] = second
            hid[2 * j + cc, rows(hh), 0:384] = third.astype(BF16)
            first, second, third = parts(jnp.where(low, tail, other), jnp.where(low, other, tail))
            ab[2 * j + cc, rows(hh), 768:896] = jnp.where(low, first, second)
            hid[2 * j + cc, rows(hh), 384:512] = third.astype(BF16)

    a_step(1)
    a_step(2)
    b_step(1)
    a_step(3)
    partial_of(0)
    partial_of(1)
    partial_of(-1)
    a_step(4)
    b_step(2)
    for k in (2, -2, 3, -3, 4 - 8):
        if k == -4:
            a_core[(4, 1)].wait_recv()
            a_core[(-4, 0)].wait_recv()
            partial(4)
        else:
            partial_of(k)

    n_x.wait_recv()
    n_block = normed.at[2 * z + c]
    n_got = {1: send(n_block, n_block, z_next), -1: send(n_block, n_block, z_prev)}
    n_core = [send(n_block, n_block, c_mate)]

    def n_step(k):
        after = {}
        for way in (1, -1):
            if way not in n_got:
                continue
            n_got[way].wait_recv()
            block = normed.at[2 * at_z(-way * k) + c]
            half = block.at[0:48] if way == 1 else block.at[48:96]
            if k == 4:
                block = half
            to = z_next if way == 1 else z_prev
            if k < 3:
                after[way] = send(block, block, to)
            elif k == 3:
                after[way] = send(half, half, to)
            n_core.append(send(block, block, c_mate))
        n_got.clear()
        n_got.update(after)

    j4 = at_y(4)
    up_got = send(part.at[j4, 0:48], crp.at[0, 0:48], y_next)
    down_got = send(part.at[j4, 48:96], crm.at[0, 48:96], y_prev)
    b_step(3)
    for s in (1, 2, 3):
        if s == 1:
            n_step(1)
        up_got.wait_recv()
        j = at_y(4 - s)
        span = slice(0, 48) if s == 1 else slice(0, 96)
        part[j, span] = (part[j, span].astype(F32) + crp[s - 1, span].astype(F32)).astype(BF16)
        up_got = send(part.at[j], crp.at[s], y_next)
        down_got.wait_recv()
        j = at_y(s - 4)
        span = slice(48, 96) if s == 1 else slice(0, 96)
        part[j, span] = (part[j, span].astype(F32) + crm[s - 1, span].astype(F32)).astype(BF16)
        down_got = send(part.at[j], crm.at[s], y_prev)
        if s == 1:
            b_step(4)
            n_step(2)
            for k in range(0, 4):
                factors(xl * 8 + at_y(k))
        elif s == 2:
            n_step(3)
            for k in range(4, 8):
                factors(xl * 8 + at_y(k))
    up_got.wait_recv()
    down_got.wait_recv()
    part[y] = (part[y].astype(F32) + crp[3].astype(F32) + crm[3].astype(F32)).astype(BF16)
    x_got = send(part.at[y], xr, x_mate)
    n_step(4)
    x_got.wait_recv()
    hg[y] = (part[y].astype(F32) + xr[...].astype(F32)).astype(BF16)

    d_got = {1: send(hg.at[y], hg.at[y], y_next), -1: send(hg.at[y], hg.at[y], y_prev)}

    for copy in b_x:
        copy.wait_recv()

    def other_factors(k, carry):
        factors((1 - xl) * 8 + (y + k) % 8)
        return carry

    lax.fori_loop(0, 8, other_factors, 0)

    e_core = {}

    def back(k):
        j = at_y(k)
        block = hg[j].astype(F32)
        tail = block[:, 768:896]
        other = swap(tail)
        for cc in (0, 1):
            main = block[:, 384 * cc : 384 * cc + 384]
            both = jnp.where(low96, tail, other) if cc == 0 else jnp.where(low96, other, tail)
            gu[2 * j + cc, :, 0:384] = (ab[2 * j + cc, :, 0:384] * main).astype(BF16)
            gu[2 * j + cc, :, 384:768] = (ab[2 * j + cc, :, 384:768] * main).astype(BF16)
            gu[2 * j + cc, :, 768:896] = (ab[2 * j + cc, :, 768:896] * both).astype(BF16)
        value = dot(gu[pl.ds(2 * j, 2)].reshape(192, 896), wgu[...], 1, 1).astype(BF16)
        igp[2 * j] = value[0:96]
        igp[2 * j + 1] = value[96:192]
        e_core[k] = send(igp.at[2 * j + 1 - c], xc.at[j], c_mate)

    def d_step(k):
        after = {}
        for way in (1, -1):
            if way not in d_got:
                continue
            d_got[way].wait_recv()
            block = hg.at[at_y(-way * k)]
            half = block.at[0:48] if way == 1 else block.at[48:96]
            to = y_next if way == 1 else y_prev
            if k < 3:
                after[way] = send(block, block, to)
            elif k == 3:
                after[way] = send(half, half, to)
        d_got.clear()
        d_got.update(after)

    back(0)
    d_step(1)
    back(1)
    back(-1)
    for copy in n_core:
        copy.wait_recv()
    for m in range(4):
        cols = slice(128 * m, 128 * m + 128)
        nt[cols, :] = normed[:, :, cols].reshape(1536, 128).T
    d_step(2)
    back(2)
    back(-2)
    for m in range(2):
        cols = slice(256 * m, 256 * m + 256)
        value = dot(hid[:, :, cols].reshape(1536, 256), grads[...].reshape(1536, 512), 0, 0)
        size = 256 if m == 0 else 192
        dwg_ref[256 * m : 256 * m + size, :] = value[0:size].astype(BF16)
    d_step(3)
    back(3)
    back(-3)
    d_step(4)
    back(4)

    for copy in e_core.values():
        copy.wait_recv()

    def mine(j, span):
        return igp[2 * j + c, span].astype(F32) + xc[j, span].astype(F32)

    def weight_grads(m):
        value = dot(nt[128 * m : 128 * m + 128, :], gu[...].reshape(1536, 896), 1, 0).astype(BF16)
        span = slice(128 * m, 128 * m + 128)
        gwg_ref[span, 0:384] = value[:, 0:384]
        gwg_ref[span, 384:448] = value[:, 768:832]
        uwg_ref[span, 0:384] = value[:, 384:768]
        uwg_ref[span, 384:448] = value[:, 832:896]

    j4 = at_z(4)
    es[j4] = mine(j4, slice(0, 96)).astype(BF16)
    up_got = send(es.at[j4, 0:48], erp.at[0, 0:48], z_next)
    down_got = send(es.at[j4, 48:96], erm.at[0, 48:96], z_prev)
    weight_grads(0)
    for s in (1, 2, 3):
        up_got.wait_recv()
        j = at_z(4 - s)
        if s == 1:
            es[j, 0:48] = (mine(j, slice(0, 48)) + erp[0, 0:48].astype(F32)).astype(BF16)
            es[j, 48:96] = mine(j, slice(48, 96)).astype(BF16)
        else:
            es[j] = (mine(j, slice(0, 96)) + erp[s - 1].astype(F32)).astype(BF16)
        up_got = send(es.at[j], erp.at[s], z_next)
        down_got.wait_recv()
        j = at_z(s - 4)
        if s == 1:
            es[j, 48:96] = (mine(j, slice(48, 96)) + erm[0, 48:96].astype(F32)).astype(BF16)
            es[j, 0:48] = mine(j, slice(0, 48)).astype(BF16)
        else:
            es[j] = (mine(j, slice(0, 96)) + erm[s - 1].astype(F32)).astype(BF16)
        down_got = send(es.at[j], erm.at[s], z_prev)
        weight_grads(s)
    up_got.wait_recv()
    down_got.wait_recv()
    total = mine(z, slice(0, 96)) + erp[3].astype(F32) + erm[3].astype(F32)
    es[z] = total.astype(BF16)
    last = send(es.at[z, rows(1 - h)], eh, h_mate)
    for copy in started:
        copy.wait_send()
    last.wait_recv()
    ig_ref[...] = (es[z, rows(h), :].astype(F32) + eh[...].astype(F32)).astype(BF16)


COPIES = 160


def shards(*operands):
    vmem = pl.BlockSpec(memory_space=pltpu.VMEM)
    shapes = [
        ((16, 96, 512), BF16),
        ((16, 96, 512), BF16),
        ((16, 96, 896), BF16),
        ((8, 96, 896), BF16),
        ((4, 96, 896), BF16),
        ((4, 96, 896), BF16),
        ((96, 896), BF16),
        ((8, 96, 896), BF16),
        ((16, 96, 896), F32),
        ((16, 96, 512), BF16),
        ((16, 96, 896), BF16),
        ((16, 96, 512), BF16),
        ((8, 96, 512), BF16),
        ((8, 96, 512), BF16),
        ((4, 96, 512), BF16),
        ((4, 96, 512), BF16),
        ((48, 512), BF16),
        ((512, 896), BF16),
        ((512, 512), BF16),
        ((512, 1536), BF16),
    ]
    return pl.pallas_call(
        kernel,
        out_shape=(
            jax.ShapeDtypeStruct((48, 512), BF16),
            jax.ShapeDtypeStruct((512, 448), BF16),
            jax.ShapeDtypeStruct((512, 448), BF16),
            jax.ShapeDtypeStruct((448, 512), BF16),
        ),
        in_specs=[vmem] * 9,
        out_specs=(vmem,) * 4,
        scratch_shapes=[pltpu.VMEM(shape, kind) for shape, kind in shapes]
        + [pltpu.SemaphoreType.DMA((COPIES,)), pltpu.SemaphoreType.DMA((COPIES,))],
        compiler_params=pltpu.CompilerParams(
            collective_id=0, has_side_effects=True, vmem_limit_bytes=48 * 1024 * 1024
        ),
    )(*operands, hadamard(BLOCK))


def solution(mesh):
    return jax.shard_map(
        shards,
        mesh=mesh,
        in_specs=(
            P("tensor", "dp"),
            P("tensor", "dp"),
            P("tensor", "dp"),
            P("dp", "tensor"),
            P("dp", "tensor"),
            P("dp", "tensor"),
            P("dp", "tensor"),
            P("tensor", "dp"),
        ),
        out_specs=(P("tensor", "dp"), P("dp", "tensor"), P("dp", "tensor"), P("tensor", "dp")),
        check_vma=False,
    )
```

```python
import jax
import jax.numpy as jnp
from jax import lax
from jax.experimental import pallas as pl
from jax.experimental.pallas import tpu as pltpu
from jax.sharding import PartitionSpec as P

BLOCK = 128
MESH = pl.DeviceIdType.MESH
F32 = jnp.float32
BF16 = jnp.bfloat16


def hadamard():
    common = lax.broadcasted_iota(jnp.int32, (BLOCK, BLOCK), 0) & lax.broadcasted_iota(
        jnp.int32, (BLOCK, BLOCK), 1
    )
    for shift in (4, 2, 1):
        common = common ^ (common >> shift)
    return (1 - 2 * (common & 1)).astype(F32).astype(BF16)


def dot(left, right, left_dim, right_dim):
    return lax.dot_general(
        left, right, (((left_dim,), (right_dim,)), ((), ())), preferred_element_type=F32
    )


def kernel(
    grad_ref, rot_ref, scale_ref, gate_ref, up_ref, gw_ref, uw_ref, dw_ref,
    ig_ref, gwg_ref, uwg_ref, dwg_ref,
    grads, normed, ug, part, crp, crm, xr, hg, ab, hid, gu, igp, xc, es, erp, erm, eap, eam, eh,
    wgu, dwp, rot, scale, gate, up, load_sem, send_sem, recv_sem,
):
    d = lax.axis_index("dp")
    t = lax.axis_index("tensor")
    xl, y = d // 8, d % 8
    z, h, c = t // 4, (t // 2) % 2, t % 2

    def at_y(k):
        return (y + (k + 8)) % 8

    def at_z(k):
        return (z + (k + 8)) % 8

    def y_to(k):
        return {"dp": xl * 8 + at_y(k)}

    def z_to(k, column=h):
        return {"tensor": at_z(k) * 4 + column * 2 + c}

    x_mate = {"dp": (1 - xl) * 8 + y}
    h_mate = z_to(0, 1 - h)
    c_mate = {"tensor": z * 4 + h * 2 + (1 - c)}

    barrier = pltpu.get_barrier_semaphore()
    partners = [z_to(1), z_to(-1), z_to(1, 1 - h), z_to(-1, 1 - h), h_mate, c_mate]
    partners += [y_to(1), y_to(-1), x_mate, z_to(2), z_to(-2), z_to(2, 1 - h), z_to(-2, 1 - h)]
    for other in partners:
        pl.semaphore_signal(barrier, inc=1, device_id=other, device_id_type=MESH)

    def rows(half):
        return pl.ds(pl.multiple_of(half * 48, 16), 48)

    loads = []

    def load(src, dst):
        copy = pltpu.make_async_copy(src, dst, load_sem.at[len(loads)])
        copy.start()
        loads.append(copy)
        return copy

    own_piece = grads.at[2 * z + c, rows(h)]
    got_grad = load(grad_ref, own_piece)
    got_gate = [load(gate_ref, gate), load(up_ref, up)]
    got_rot = [load(rot_ref, rot), load(scale_ref, scale)]
    got_dw = load(dw_ref, dwp.at[0:448])
    got_w = [
        load(gw_ref.at[0:384], wgu.at[0:384]),
        load(uw_ref.at[0:384], wgu.at[384:768]),
        load(gw_ref.at[384:448], wgu.at[768:832]),
        load(uw_ref.at[384:448], wgu.at[832:896]),
    ]

    started = []

    def send(src, dst, to):
        index = len(started)
        copy = pltpu.make_async_remote_copy(
            src_ref=src,
            dst_ref=dst,
            send_sem=send_sem.at[index],
            recv_sem=recv_sem.at[index],
            device_id=to,
            device_id_type=MESH,
        )
        copy.start()
        started.append(copy)
        return copy

    low = lax.broadcasted_iota(jnp.int32, (48, 128), 1) < 64
    low96 = lax.broadcasted_iota(jnp.int32, (96, 128), 1) < 64

    def swap(value):
        return pltpu.roll(value, 64, 1)

    dwp[448:512, :] = jnp.zeros((64, 512), BF16)
    got_grad.wait()

    pl.semaphore_wait(barrier, len(partners))

    a_core = {}
    a_got = {}
    for k in (2, -2):
        for column in (0, 1):
            a_got[(k, column)] = send(own_piece, own_piece, z_to(k, h if column == 0 else 1 - h))
    a_x = send(own_piece, own_piece, h_mate)
    for k in (1, -1):
        for column in (0, 1):
            a_got[(k, column)] = send(own_piece, own_piece, z_to(k, h if column == 0 else 1 - h))

    for copy in got_gate:
        copy.wait()
    ug[d, :, 0:384] = gate[:, 0:384]
    ug[d, :, 384:768] = up[:, 0:384]
    ug[d, :, 768:896] = jnp.concatenate([gate[:, 384:448], up[:, 384:448]], axis=1)
    b_x = []
    q = (slice(0, 48), slice(48, 96))
    b_got = {}
    for half in (0, 1):
        for way in (1, -1):
            piece = ug.at[d, q[half if way == 1 else 1 - half]]
            b_got[(way, half if way == 1 else 1 - half)] = send(piece, piece, y_to(way))

    for copy in got_rot:
        copy.wait()
    table = hadamard()
    eye = lax.broadcasted_iota(jnp.int32, (48, 48), 0) == lax.broadcasted_iota(
        jnp.int32, (48, 48), 1
    )
    for b in range(4):
        cols = slice(128 * b, 128 * b + 128)
        mixed = dot(rot[:, cols], table, 1, 0)
        row = jnp.broadcast_to(scale[b : b + 1, :], (48, 48))
        column = jnp.sum(jnp.where(eye, row, 0.0), axis=1, keepdims=True)
        normed[2 * z + c, rows(h), cols] = (mixed * (column * BLOCK ** (-0.5))).astype(BF16)
    own_normed = normed.at[2 * z + c, rows(h)]
    n_x = send(own_normed, own_normed, h_mate)
    got_dw.wait()

    def a_share(k):
        block = grads.at[2 * at_z(k) + c]
        a_core[k] = send(block, block, c_mate)

    for way in (1, -1):
        for column in (0, 1):
            a_got[(2 * way, column)].wait_recv()
        block = grads.at[2 * at_z(-2 * way) + c]
        a_got[(3 * way, 0)] = send(block, block, z_to(way))
        piece = block.at[0:48] if way == 1 else block.at[48:96]
        a_got[(4 * way, 0)] = send(piece, piece, z_to(2 * way))
    a_x.wait_recv()
    a_share(0)
    for way in (1, -1):
        for column in (0, 1):
            a_got[(way, column)].wait_recv()
        a_share(-way)
    for way in (1, -1):
        a_share(-2 * way)

    def b_step(k):
        for first in (True, False):
            for way in (1, -1):
                half = 0 if (way == 1) == first else 1
                if k == 4 and not first:
                    continue
                b_got[(way, half)].wait_recv()
                piece = ug.at[xl * 8 + at_y(-way * k), q[half]]
                if k < 3 or (k == 3 and first):
                    b_got[(way, half)] = send(piece, piece, y_to(way))
        for way in (1, -1) if k < 4 else ():
            block = ug.at[xl * 8 + at_y(-way * k)]
            b_x.append(send(block, block, x_mate))

    def partial(k):
        a_core[k].wait_recv()
        j = at_z(k)
        value = dot(grads[pl.ds(2 * j, 2)].reshape(192, 512), dwp[...], 1, 1)
        first, second = value[0:96], value[96:192]
        part[j, :, 0:384] = first[:, 0:384].astype(BF16)
        part[j, :, 384:768] = second[:, 0:384].astype(BF16)
        tail = jnp.where(low96, first[:, 384:512], swap(second[:, 384:512]))
        part[j, :, 768:896] = tail.astype(BF16)

    def factors(e):
        j, hh = e // 2, e % 2
        for cc in (0, 1):
            tile = ug[e, 48 * cc : 48 * cc + 48, :].astype(F32)
            tail = tile[:, 768:896]
            other = swap(tail)

            def parts(g, u):
                s = 1.0 / (1.0 + jnp.exp(-g))
                act = g * s
                return (u * s) * (1.0 + g * (1.0 - s)), act, act * u

            first, second, third = parts(tile[:, 0:384], tile[:, 384:768])
            ab[2 * j + cc, rows(hh), 0:384] = first
            ab[2 * j + cc, rows(hh), 384:768] = second
            hid[2 * j + cc, rows(hh), 0:384] = third.astype(BF16)
            first, second, third = parts(jnp.where(low, tail, other), jnp.where(low, other, tail))
            ab[2 * j + cc, rows(hh), 768:896] = jnp.where(low, first, second)
            hid[2 * j + cc, rows(hh), 384:512] = third.astype(BF16)

    b_x.append(send(ug.at[d], ug.at[d], x_mate))
    b_step(1)
    for k in (0, 1, -1):
        partial(k)
    b_step(2)
    for k in (2, -2):
        partial(k)
    for way in (1, -1):
        a_got[(3 * way, 0)].wait_recv()
        a_share(-3 * way)
    for way in (1, -1):
        a_got[(4 * way, 0)].wait_recv()
    a_share(4)
    for k in (3, -3, 4):
        partial(k)

    boxes = {1: crp, -1: crm}
    c_got = {}

    def c_send(way, half, hop):
        c_got[(way, half, hop)] = send(
            part.at[at_y(way * (4 - hop)), q[half]], boxes[way].at[hop, q[half]], y_to(way)
        )

    def c_add(way, half, hop):
        c_got[(way, half, hop - 1)].wait_recv()
        j = at_y(way * (4 - hop))
        came = boxes[way][hop - 1, q[half], :].astype(F32)
        part[j, q[half], :] = (part[j, q[half], :].astype(F32) + came).astype(BF16)

    long_half = {1: 0, -1: 1}
    for way in (1, -1):
        c_send(way, long_half[way], 0)
    for way in (1, -1):
        c_send(way, 1 - long_half[way], 1)

    n_x.wait_recv()
    n_block = normed.at[2 * z + c]
    n_got = {1: send(n_block, n_block, z_to(1)), -1: send(n_block, n_block, z_to(-1))}
    n_core = [send(n_block, n_block, c_mate)]

    def n_step(k):
        after = {}
        for way in (1, -1):
            if way not in n_got:
                continue
            n_got[way].wait_recv()
            block = normed.at[2 * at_z(-way * k) + c]
            half = block.at[0:48] if way == 1 else block.at[48:96]
            if k == 4:
                block = half
            if k < 3:
                after[way] = send(block, block, z_to(way))
            elif k == 3:
                after[way] = send(half, half, z_to(way))
            n_core.append(send(block, block, c_mate))
        n_got.clear()
        n_got.update(after)

    for hop in (1, 2, 3):
        for way in (1, -1):
            c_add(way, long_half[way], hop)
            c_send(way, long_half[way], hop)
        if hop < 3:
            for way in (1, -1):
                c_add(way, 1 - long_half[way], hop + 1)
                c_send(way, 1 - long_half[way], hop + 1)
        if hop == 1:
            b_step(3)
            n_step(1)
            for k in range(0, 3):
                factors(xl * 8 + at_y(k))
        elif hop == 2:
            b_step(4)
            n_step(2)
            for k in (3, 5):
                factors(xl * 8 + at_y(k))
    x_got = {}
    for half in (1, 0):
        c_got[(1, half, 3)].wait_recv()
        c_got[(-1, half, 3)].wait_recv()
        total = part[y, q[half], :].astype(F32) + crp[3, q[half], :].astype(F32)
        part[y, q[half], :] = (total + crm[3, q[half], :].astype(F32)).astype(BF16)
        x_got[half] = send(part.at[y, q[half]], xr.at[q[half]], x_mate)
    block = ug.at[xl * 8 + at_y(4)]
    b_x.append(send(block, block, x_mate))
    d_got = {}
    for half in (1, 0):
        x_got[half].wait_recv()
        total = part[y, q[half], :].astype(F32) + xr[q[half], :].astype(F32)
        hg[y, q[half], :] = total.astype(BF16)
        for way in (1, -1):
            d_got[(way, half)] = send(hg.at[y, q[half]], hg.at[y, q[half]], y_to(way))

    n_step(3)
    for k in (4, 6, 7):
        factors(xl * 8 + at_y(k))
    def other_factors(k, carry):
        factors((1 - xl) * 8 + (y + k) % 8)
        return carry

    e_core = {}

    def back(k):
        j = at_y(k)
        block = hg[j].astype(F32)
        tail = block[:, 768:896]
        other = swap(tail)
        for cc in (0, 1):
            main = block[:, 384 * cc : 384 * cc + 384]
            both = jnp.where(low96, tail, other) if cc == 0 else jnp.where(low96, other, tail)
            gu[2 * j + cc, :, 0:384] = (ab[2 * j + cc, :, 0:384] * main).astype(BF16)
            gu[2 * j + cc, :, 384:768] = (ab[2 * j + cc, :, 384:768] * main).astype(BF16)
            gu[2 * j + cc, :, 768:896] = (ab[2 * j + cc, :, 768:896] * both).astype(BF16)
        value = dot(gu[pl.ds(2 * j, 2)].reshape(192, 896), wgu[...], 1, 0).astype(BF16)
        igp[2 * j] = value[0:96]
        igp[2 * j + 1] = value[96:192]
        e_core[k] = send(igp.at[2 * j + 1 - c], xc.at[j], c_mate)

    def d_step(k):
        for first in (True, False):
            for way in (1, -1):
                half = long_half[way] if first else 1 - long_half[way]
                if k == 4 and not first:
                    continue
                d_got[(way, half)].wait_recv()
                piece = hg.at[at_y(-way * k), q[half]]
                if k < 3 or (k == 3 and first):
                    d_got[(way, half)] = send(piece, piece, y_to(way))

    d_step(1)
    for copy in b_x[0:5]:
        copy.wait_recv()
    lax.fori_loop(0, 3, other_factors, 0)
    lax.fori_loop(6, 8, other_factors, 0)
    d_step(2)
    for copy in b_x[5:8]:
        copy.wait_recv()
    lax.fori_loop(3, 6, other_factors, 0)
    for copy in got_w:
        copy.wait()
    d_step(3)
    for k in (0, 1, -1, 2, -2):
        back(k)
    n_step(4)
    back(3)
    back(-3)
    d_step(4)
    back(4)

    for copy in e_core.values():
        copy.wait_recv()

    def mine(j, span):
        return igp[2 * j + c, span, :].astype(F32) + xc[j, span, :].astype(F32)

    def weight_grads(m):
        cols = slice(128 * m, 128 * m + 128)
        value = dot(gu[:, :, cols].reshape(1536, 128), normed[...].reshape(1536, 512), 0, 0)
        value = value.astype(BF16)
        if m < 3:
            gwg_ref[cols, :] = value
        elif m < 6:
            uwg_ref[128 * (m - 3) : 128 * (m - 2), :] = value
        else:
            gwg_ref[384:448, :] = value[0:64]
            uwg_ref[384:448, :] = value[64:128]

    spans = (rows(h), rows(1 - h))
    boxes_e = {1: erp, -1: erm}
    e_far = {}
    e_got = {}
    def down_grads(m):
        cols = slice(256 * m, 256 * m + 256)
        value = dot(hid[:, :, cols].reshape(1536, 256), grads[...].reshape(1536, 512), 0, 0)
        size = 256 if m == 0 else 192
        dwg_ref[256 * m : 256 * m + size, :] = value[0:size].astype(BF16)

    j4 = at_z(4)
    es[z, spans[1], :] = mine(z, spans[1]).astype(BF16)
    for way, column, box in ((1, 1, eap), (-1, 0, eam)):
        es[j4, spans[column], :] = mine(j4, spans[column]).astype(BF16)
        e_far[way] = send(es.at[j4, spans[column]], box, z_to(2 * way))
    for hop in (0, 1, 2):
        for column in (1, 0):
            for way in (1, -1):
                j = at_z(way * (3 - hop))
                span = spans[column]
                value = mine(j, span)
                if hop > 0:
                    e_got[(way, column)].wait_recv()
                    value = value + boxes_e[way][hop - 1, span, :].astype(F32)
                if hop == 1 and way == (1 if column == 1 else -1):
                    e_far[way].wait_recv()
                    value = value + (eap if way == 1 else eam)[...].astype(F32)
                es[j, span, :] = value.astype(BF16)
                if hop == 2 and column == 1:
                    box = eh.at[0 if way == 1 else 1]
                    e_got[(way, 1)] = send(es.at[j, span], box, z_to(way, 1 - h))
                else:
                    box = boxes_e[way].at[hop, span]
                    e_got[(way, column)] = send(es.at[j, span], box, z_to(way))
        if hop == 0:
            e_mate = send(es.at[z, spans[1]], eh.at[2], h_mate)
            down_grads(0)
            for copy in n_core:
                copy.wait_recv()
            weight_grads(0)
        else:
            for m in range(3 * hop - 2, 3 * hop + 1):
                weight_grads(m)
    down_grads(1)

    total = mine(z, spans[0])
    for way in (1, -1):
        e_got[(way, 0)].wait_recv()
        total = total + boxes_e[way][2, spans[0], :].astype(F32)
    e_mate.wait_recv()
    total = total + eh[2].astype(F32)
    for copy in started:
        copy.wait_send()
    for way in (1, -1):
        e_got[(way, 1)].wait_recv()
    ig_ref[...] = (total + (eh[0].astype(F32) + eh[1].astype(F32))).astype(BF16)


COPIES = 220


def shards(grad_out, rot, scale, gate, up, gate_weight, up_weight, down_weight):
    vmem = pl.BlockSpec(memory_space=pltpu.VMEM)
    shapes = [
        ((16, 96, 512), BF16),
        ((16, 96, 512), BF16),
        ((16, 96, 896), BF16),
        ((8, 96, 896), BF16),
        ((4, 96, 896), BF16),
        ((4, 96, 896), BF16),
        ((96, 896), BF16),
        ((8, 96, 896), BF16),
        ((16, 96, 896), F32),
        ((16, 96, 512), BF16),
        ((16, 96, 896), BF16),
        ((16, 96, 512), BF16),
        ((8, 96, 512), BF16),
        ((8, 96, 512), BF16),
        ((3, 96, 512), BF16),
        ((3, 96, 512), BF16),
        ((48, 512), BF16),
        ((48, 512), BF16),
        ((3, 48, 512), BF16),
        ((896, 512), BF16),
        ((512, 512), BF16),
        ((48, 512), BF16),
        ((4, 48), F32),
        ((96, 448), BF16),
        ((96, 448), BF16),
    ]
    ig, gwg, uwg, dwg = pl.pallas_call(
        kernel,
        out_shape=(
            jax.ShapeDtypeStruct((48, 512), BF16),
            jax.ShapeDtypeStruct((448, 512), BF16),
            jax.ShapeDtypeStruct((448, 512), BF16),
            jax.ShapeDtypeStruct((448, 512), BF16),
        ),
        in_specs=[pl.BlockSpec(memory_space=pl.ANY)] * 8,
        out_specs=(vmem,) * 4,
        scratch_shapes=[pltpu.VMEM(shape, kind) for shape, kind in shapes]
        + [
            pltpu.SemaphoreType.DMA((16,)),
            pltpu.SemaphoreType.DMA((COPIES,)),
            pltpu.SemaphoreType.DMA((COPIES,)),
        ],
        compiler_params=pltpu.CompilerParams(
            collective_id=0, has_side_effects=True, vmem_limit_bytes=60 * 1024 * 1024
        ),
    )(grad_out, rot, scale.T, gate, up, gate_weight.T, up_weight.T, down_weight)
    return ig, gwg.T, uwg.T, dwg


def solution(mesh):
    return jax.shard_map(
        shards,
        mesh=mesh,
        in_specs=(
            P("tensor", "dp"),
            P("tensor", "dp"),
            P("tensor", "dp"),
            P("dp", "tensor"),
            P("dp", "tensor"),
            P("dp", "tensor"),
            P("dp", "tensor"),
            P("tensor", "dp"),
        ),
        out_specs=(P("tensor", "dp"), P("dp", "tensor"), P("dp", "tensor"), P("tensor", "dp")),
        check_vma=False,
    )
```

```python
import jax
import jax.numpy as jnp
from jax import lax
from jax.experimental import pallas as pl
from jax.experimental.pallas import tpu as pltpu
from jax.sharding import PartitionSpec as P

BLOCK = 128
MESH = pl.DeviceIdType.MESH
F32 = jnp.float32
BF16 = jnp.bfloat16


def hadamard():
    common = lax.broadcasted_iota(jnp.int32, (BLOCK, BLOCK), 0) & lax.broadcasted_iota(
        jnp.int32, (BLOCK, BLOCK), 1
    )
    for shift in (4, 2, 1):
        common = common ^ (common >> shift)
    return (1 - 2 * (common & 1)).astype(F32).astype(BF16)


def dot(left, right, left_dim, right_dim):
    return lax.dot_general(
        left, right, (((left_dim,), (right_dim,)), ((), ())), preferred_element_type=F32
    )


def kernel(
    grad_ref, rot_ref, scale_ref, gate_ref, up_ref, gw_ref, uw_ref, dw_ref,
    ig_ref, gwg_ref, uwg_ref, dwg_ref,
    grads, normed, ug, part, crp, crm, xr, hg, ab, hid, gu, igp, xc, es, erp, erm, eap, eam, eh,
    wgu, dwp, rot, scale, gate, up, load_sem, send_sem, recv_sem,
):
    d = lax.axis_index("dp")
    t = lax.axis_index("tensor")
    xl, y = d // 8, d % 8
    z, h, c = t // 4, (t // 2) % 2, t % 2

    def at_y(k):
        return (y + (k + 8)) % 8

    def at_z(k):
        return (z + (k + 8)) % 8

    def y_to(k):
        return {"dp": xl * 8 + at_y(k)}

    def z_to(k, column=h):
        return {"tensor": at_z(k) * 4 + column * 2 + c}

    x_mate = {"dp": (1 - xl) * 8 + y}
    h_mate = z_to(0, 1 - h)
    c_mate = {"tensor": z * 4 + h * 2 + (1 - c)}

    barrier = pltpu.get_barrier_semaphore()
    partners = [z_to(1), z_to(-1), z_to(1, 1 - h), z_to(-1, 1 - h), h_mate, c_mate]
    partners += [y_to(1), y_to(-1), x_mate, z_to(2), z_to(-2), z_to(2, 1 - h), z_to(-2, 1 - h)]
    for other in partners:
        pl.semaphore_signal(barrier, inc=1, device_id=other, device_id_type=MESH)

    def rows(half):
        return pl.ds(pl.multiple_of(half * 48, 16), 48)

    loads = []

    def load(src, dst):
        copy = pltpu.make_async_copy(src, dst, load_sem.at[len(loads)])
        copy.start()
        loads.append(copy)
        return copy

    own_piece = grads.at[2 * z + c, rows(h)]
    got_grad = load(grad_ref, own_piece)
    got_gate = [load(gate_ref, gate), load(up_ref, up)]
    got_rot = [load(rot_ref, rot), load(scale_ref, scale)]
    got_dw = load(dw_ref, dwp.at[0:448])
    got_w = [
        load(gw_ref.at[0:384], wgu.at[0:384]),
        load(uw_ref.at[0:384], wgu.at[384:768]),
        load(gw_ref.at[384:448], wgu.at[768:832]),
        load(uw_ref.at[384:448], wgu.at[832:896]),
    ]

    started = []

    def send(src, dst, to):
        index = len(started)
        copy = pltpu.make_async_remote_copy(
            src_ref=src,
            dst_ref=dst,
            send_sem=send_sem.at[index],
            recv_sem=recv_sem.at[index],
            device_id=to,
            device_id_type=MESH,
        )
        copy.start()
        started.append(copy)
        return copy

    low = lax.broadcasted_iota(jnp.int32, (48, 128), 1) < 64
    low96 = lax.broadcasted_iota(jnp.int32, (96, 128), 1) < 64

    def swap(value):
        return pltpu.roll(value, 64, 1)

    dwp[448:512, :] = jnp.zeros((64, 512), BF16)
    got_grad.wait()

    pl.semaphore_wait(barrier, len(partners))

    a_core = {}
    a_got = {}
    for k in (2, -2):
        for column in (0, 1):
            a_got[(k, column)] = send(own_piece, own_piece, z_to(k, h if column == 0 else 1 - h))
    a_x = send(own_piece, own_piece, h_mate)
    for k in (1, -1):
        for column in (0, 1):
            a_got[(k, column)] = send(own_piece, own_piece, z_to(k, h if column == 0 else 1 - h))

    for copy in got_gate:
        copy.wait()
    ug[d, :, 0:384] = gate[:, 0:384]
    ug[d, :, 384:768] = up[:, 0:384]
    ug[d, :, 768:896] = jnp.concatenate([gate[:, 384:448], up[:, 384:448]], axis=1)
    b_x = []
    q = (slice(0, 48), slice(48, 96))
    b_got = {}
    for half in (0, 1):
        for way in (1, -1):
            piece = ug.at[d, q[half if way == 1 else 1 - half]]
            b_got[(way, half if way == 1 else 1 - half)] = send(piece, piece, y_to(way))

    for copy in got_rot:
        copy.wait()
    table = hadamard()
    eye = lax.broadcasted_iota(jnp.int32, (48, 48), 0) == lax.broadcasted_iota(
        jnp.int32, (48, 48), 1
    )
    for b in range(4):
        cols = slice(128 * b, 128 * b + 128)
        mixed = dot(rot[:, cols], table, 1, 0)
        row = jnp.broadcast_to(scale[b : b + 1, :], (48, 48))
        column = jnp.sum(jnp.where(eye, row, 0.0), axis=1, keepdims=True)
        normed[2 * z + c, rows(h), cols] = (mixed * (column * BLOCK ** (-0.5))).astype(BF16)
    own_normed = normed.at[2 * z + c, rows(h)]
    n_x = send(own_normed, own_normed, h_mate)
    got_dw.wait()

    def a_share(k):
        block = grads.at[2 * at_z(k) + c]
        a_core[k] = send(block, block, c_mate)

    for way in (1, -1):
        for column in (0, 1):
            a_got[(2 * way, column)].wait_recv()
        block = grads.at[2 * at_z(-2 * way) + c]
        a_got[(3 * way, 0)] = send(block, block, z_to(way))
        piece = block.at[0:48] if way == 1 else block.at[48:96]
        a_got[(4 * way, 0)] = send(piece, piece, z_to(2 * way))
    a_x.wait_recv()
    a_share(0)
    for way in (1, -1):
        for column in (0, 1):
            a_got[(way, column)].wait_recv()
        a_share(-way)
    for way in (1, -1):
        a_share(-2 * way)

    def b_step(k):
        for first in (True, False):
            for way in (1, -1):
                half = 0 if (way == 1) == first else 1
                if k == 4 and not first:
                    continue
                b_got[(way, half)].wait_recv()
                piece = ug.at[xl * 8 + at_y(-way * k), q[half]]
                if k < 3 or (k == 3 and first):
                    b_got[(way, half)] = send(piece, piece, y_to(way))
        for way in (1, -1) if k < 4 else ():
            block = ug.at[xl * 8 + at_y(-way * k)]
            b_x.append(send(block, block, x_mate))

    def partial(k):
        a_core[k].wait_recv()
        j = at_z(k)
        value = dot(grads[pl.ds(2 * j, 2)].reshape(192, 512), dwp[...], 1, 1)
        first, second = value[0:96], value[96:192]
        part[j, :, 0:384] = first[:, 0:384].astype(BF16)
        part[j, :, 384:768] = second[:, 0:384].astype(BF16)
        tail = jnp.where(low96, first[:, 384:512], swap(second[:, 384:512]))
        part[j, :, 768:896] = tail.astype(BF16)

    def factors(e):
        j, hh = e // 2, e % 2
        for cc in (0, 1):
            tile = ug[e, 48 * cc : 48 * cc + 48, :].astype(F32)
            tail = tile[:, 768:896]
            other = swap(tail)

            def parts(g, u):
                s = 1.0 / (1.0 + jnp.exp(-g))
                act = g * s
                return (u * s) * (1.0 + g * (1.0 - s)), act, act * u

            first, second, third = parts(tile[:, 0:384], tile[:, 384:768])
            ab[2 * j + cc, rows(hh), 0:384] = first
            ab[2 * j + cc, rows(hh), 384:768] = second
            hid[2 * j + cc, rows(hh), 0:384] = third.astype(BF16)
            first, second, third = parts(jnp.where(low, tail, other), jnp.where(low, other, tail))
            ab[2 * j + cc, rows(hh), 768:896] = jnp.where(low, first, second)
            hid[2 * j + cc, rows(hh), 384:512] = third.astype(BF16)

    b_x.append(send(ug.at[d], ug.at[d], x_mate))
    b_step(1)
    for k in (0, 1, -1):
        partial(k)
    b_step(2)
    for k in (2, -2):
        partial(k)
    for way in (1, -1):
        a_got[(3 * way, 0)].wait_recv()
        a_share(-3 * way)
    for way in (1, -1):
        a_got[(4 * way, 0)].wait_recv()
    a_share(4)
    for k in (3, -3, 4):
        partial(k)

    boxes = {1: crp, -1: crm}
    spans_c = {
        1: (slice(0, 32), slice(32, 48), slice(48, 96)),
        -1: (slice(64, 96), slice(48, 64), slice(0, 48)),
    }
    in_half = {0: ((1, 0), (1, 1), (-1, 2)), 1: ((-1, 0), (-1, 1), (1, 2))}
    c_got = {}

    def c_send(way, p, hop):
        span = spans_c[way][p]
        c_got[(way, p, hop)] = send(
            part.at[at_y(way * (4 - hop)), span], boxes[way].at[hop, span], y_to(way)
        )

    def c_add(way, p, hop):
        c_got[(way, p, hop - 1)].wait_recv()
        j = at_y(way * (4 - hop))
        span = spans_c[way][p]
        came = boxes[way][hop - 1, span, :].astype(F32)
        part[j, span, :] = (part[j, span, :].astype(F32) + came).astype(BF16)

    for p in (0, 1):
        for way in (1, -1):
            c_send(way, p, 0)
    for way in (1, -1):
        c_send(way, 2, 1)

    n_x.wait_recv()
    n_block = normed.at[2 * z + c]
    n_got = {1: send(n_block, n_block, z_to(1)), -1: send(n_block, n_block, z_to(-1))}
    n_core = [send(n_block, n_block, c_mate)]

    def n_step(k):
        after = {}
        for way in (1, -1):
            if way not in n_got:
                continue
            n_got[way].wait_recv()
            block = normed.at[2 * at_z(-way * k) + c]
            half = block.at[0:48] if way == 1 else block.at[48:96]
            if k == 4:
                block = half
            if k < 3:
                after[way] = send(block, block, z_to(way))
            elif k == 3:
                after[way] = send(half, half, z_to(way))
            n_core.append(send(block, block, c_mate))
        n_got.clear()
        n_got.update(after)

    for hop in (1, 2, 3):
        for p in (0, 1):
            for way in (1, -1):
                c_add(way, p, hop)
                c_send(way, p, hop)
        if hop < 3:
            for way in (1, -1):
                c_add(way, 2, hop + 1)
                c_send(way, 2, hop + 1)
        if hop == 1:
            b_step(3)
            n_step(1)
            for k in range(0, 3):
                factors(xl * 8 + at_y(k))
        elif hop == 2:
            b_step(4)
            n_step(2)
            for k in (3, 5):
                factors(xl * 8 + at_y(k))
    x_got = {}
    for half in (1, 0):
        for way, p in in_half[half]:
            c_got[(way, p, 3)].wait_recv()
        total = part[y, q[half], :].astype(F32) + crp[3, q[half], :].astype(F32)
        part[y, q[half], :] = (total + crm[3, q[half], :].astype(F32)).astype(BF16)
        x_got[half] = send(part.at[y, q[half]], xr.at[q[half]], x_mate)
    block = ug.at[xl * 8 + at_y(4)]
    b_x.append(send(block, block, x_mate))
    d_got = {}
    for half in (1, 0):
        x_got[half].wait_recv()
        total = part[y, q[half], :].astype(F32) + xr[q[half], :].astype(F32)
        hg[y, q[half], :] = total.astype(BF16)
        for way, p in in_half[half]:
            piece = hg.at[y, spans_c[way][p]]
            d_got[(way, p)] = send(piece, piece, y_to(way))

    n_step(3)
    for k in (4, 6, 7):
        factors(xl * 8 + at_y(k))
    def other_factors(k, carry):
        factors((1 - xl) * 8 + (y + k) % 8)
        return carry

    e_core = {}

    def back(k):
        j = at_y(k)
        block = hg[j].astype(F32)
        tail = block[:, 768:896]
        other = swap(tail)
        for cc in (0, 1):
            main = block[:, 384 * cc : 384 * cc + 384]
            both = jnp.where(low96, tail, other) if cc == 0 else jnp.where(low96, other, tail)
            gu[2 * j + cc, :, 0:384] = (ab[2 * j + cc, :, 0:384] * main).astype(BF16)
            gu[2 * j + cc, :, 384:768] = (ab[2 * j + cc, :, 384:768] * main).astype(BF16)
            gu[2 * j + cc, :, 768:896] = (ab[2 * j + cc, :, 768:896] * both).astype(BF16)
        value = dot(gu[pl.ds(2 * j, 2)].reshape(192, 896), wgu[...], 1, 0).astype(BF16)
        igp[2 * j] = value[0:96]
        igp[2 * j + 1] = value[96:192]
        e_core[k] = send(igp.at[2 * j + 1 - c], xc.at[j], c_mate)

    def d_step(k):
        for p in (0, 1, 2):
            for way in (1, -1):
                if k == 4 and p == 2:
                    continue
                d_got[(way, p)].wait_recv()
                piece = hg.at[at_y(-way * k), spans_c[way][p]]
                if k < 3 or (k == 3 and p < 2):
                    d_got[(way, p)] = send(piece, piece, y_to(way))

    d_step(1)
    for copy in b_x[0:5]:
        copy.wait_recv()
    lax.fori_loop(0, 3, other_factors, 0)
    lax.fori_loop(6, 8, other_factors, 0)
    d_step(2)
    for copy in b_x[5:8]:
        copy.wait_recv()
    lax.fori_loop(3, 6, other_factors, 0)
    for copy in got_w:
        copy.wait()
    d_step(3)
    for k in (0, 1, -1, 2, -2):
        back(k)
    n_step(4)
    back(3)
    back(-3)
    d_step(4)
    back(4)

    for copy in e_core.values():
        copy.wait_recv()

    def mine(j, span):
        return igp[2 * j + c, span, :].astype(F32) + xc[j, span, :].astype(F32)

    def weight_grads(m):
        cols = slice(128 * m, 128 * m + 128)
        value = dot(gu[:, :, cols].reshape(1536, 128), normed[...].reshape(1536, 512), 0, 0)
        value = value.astype(BF16)
        if m < 3:
            gwg_ref[cols, :] = value
        elif m < 6:
            uwg_ref[128 * (m - 3) : 128 * (m - 2), :] = value
        else:
            gwg_ref[384:448, :] = value[0:64]
            uwg_ref[384:448, :] = value[64:128]

    spans = (rows(h), rows(1 - h))
    boxes_e = {1: erp, -1: erm}
    e_far = {}
    e_got = {}
    e_near = {}
    def down_grads(m):
        cols = slice(256 * m, 256 * m + 256)
        value = dot(hid[:, :, cols].reshape(1536, 256), grads[...].reshape(1536, 512), 0, 0)
        size = 256 if m == 0 else 192
        dwg_ref[256 * m : 256 * m + size, :] = value[0:size].astype(BF16)

    j4 = at_z(4)
    es[z, spans[1], :] = mine(z, spans[1]).astype(BF16)
    for way, column, box in ((1, 1, eap), (-1, 0, eam)):
        es[j4, spans[column], :] = mine(j4, spans[column]).astype(BF16)
        e_far[way] = send(es.at[j4, spans[column]], box, z_to(2 * way))
    for hop in (0, 1):
        for column in (1, 0):
            for way in (1, -1):
                j = at_z(way * (3 - hop))
                span = spans[column]
                value = mine(j, span)
                if hop > 0:
                    e_got[(way, column)].wait_recv()
                    value = value + boxes_e[way][0, span, :].astype(F32)
                if hop == 1 and way == (1 if column == 1 else -1):
                    e_far[way].wait_recv()
                    value = value + (eap if way == 1 else eam)[...].astype(F32)
                es[j, span, :] = value.astype(BF16)
                if hop == 0:
                    box = boxes_e[way].at[0, span]
                    e_got[(way, column)] = send(es.at[j, span], box, z_to(way))
                elif column == 1:
                    box = eh.at[3 if way == 1 else 4]
                    e_got[(way, 1)] = send(es.at[j, span], box, z_to(2 * way, 1 - h))
                else:
                    box = boxes_e[way].at[2, span]
                    e_got[(way, 0)] = send(es.at[j, span], box, z_to(2 * way))
        if hop == 0:
            for column in (1, 0):
                for way in (1, -1):
                    j = at_z(way)
                    span = spans[column]
                    es[j, span, :] = mine(j, span).astype(BF16)
                    if column == 1:
                        box = eh.at[0 if way == 1 else 1]
                        e_near[(way, 1)] = send(es.at[j, span], box, z_to(way, 1 - h))
                    else:
                        box = boxes_e[way].at[1, span]
                        e_near[(way, 0)] = send(es.at[j, span], box, z_to(way))
        if hop == 0:
            e_mate = send(es.at[z, spans[1]], eh.at[2], h_mate)
            down_grads(0)
            for copy in n_core:
                copy.wait_recv()
            weight_grads(0)
        else:
            for m in range(1, 7):
                weight_grads(m)
    down_grads(1)

    total = mine(z, spans[0])
    for way in (1, -1):
        e_near[(way, 0)].wait_recv()
        e_got[(way, 0)].wait_recv()
        total = total + boxes_e[way][1, spans[0], :].astype(F32)
        total = total + boxes_e[way][2, spans[0], :].astype(F32)
    e_mate.wait_recv()
    total = total + eh[2].astype(F32)
    for copy in started:
        copy.wait_send()
    for way in (1, -1):
        e_near[(way, 1)].wait_recv()
        e_got[(way, 1)].wait_recv()
    for i in (0, 1, 3, 4):
        total = total + eh[i].astype(F32)
    ig_ref[...] = total.astype(BF16)


COPIES = 250


def shards(grad_out, rot, scale, gate, up, gate_weight, up_weight, down_weight):
    vmem = pl.BlockSpec(memory_space=pltpu.VMEM)
    shapes = [
        ((16, 96, 512), BF16),
        ((16, 96, 512), BF16),
        ((16, 96, 896), BF16),
        ((8, 96, 896), BF16),
        ((4, 96, 896), BF16),
        ((4, 96, 896), BF16),
        ((96, 896), BF16),
        ((8, 96, 896), BF16),
        ((16, 96, 896), F32),
        ((16, 96, 512), BF16),
        ((16, 96, 896), BF16),
        ((16, 96, 512), BF16),
        ((8, 96, 512), BF16),
        ((8, 96, 512), BF16),
        ((3, 96, 512), BF16),
        ((3, 96, 512), BF16),
        ((48, 512), BF16),
        ((48, 512), BF16),
        ((5, 48, 512), BF16),
        ((896, 512), BF16),
        ((512, 512), BF16),
        ((48, 512), BF16),
        ((4, 48), F32),
        ((96, 448), BF16),
        ((96, 448), BF16),
    ]
    operands = (grad_out, rot, scale.T, gate, up, gate_weight.T, up_weight.T, down_weight)
    operands = [pltpu.with_memory_space_constraint(each, pltpu.HBM) for each in operands]
    ig, gwg, uwg, dwg = pl.pallas_call(
        kernel,
        out_shape=(
            pltpu.VMEM((48, 512), BF16),
            pltpu.VMEM((448, 512), BF16),
            pltpu.VMEM((448, 512), BF16),
            pltpu.VMEM((448, 512), BF16),
        ),
        in_specs=[pl.BlockSpec(memory_space=pl.ANY)] * 8,
        out_specs=(vmem,) * 4,
        scratch_shapes=[pltpu.VMEM(shape, kind) for shape, kind in shapes]
        + [
            pltpu.SemaphoreType.DMA((16,)),
            pltpu.SemaphoreType.DMA((COPIES,)),
            pltpu.SemaphoreType.DMA((COPIES,)),
        ],
        compiler_params=pltpu.CompilerParams(
            collective_id=0, has_side_effects=True, vmem_limit_bytes=48 * 1024 * 1024
        ),
    )(*operands)
    return ig, gwg.T, uwg.T, dwg


def solution(mesh):
    return jax.shard_map(
        shards,
        mesh=mesh,
        in_specs=(
            P("tensor", "dp"),
            P("tensor", "dp"),
            P("tensor", "dp"),
            P("dp", "tensor"),
            P("dp", "tensor"),
            P("dp", "tensor"),
            P("dp", "tensor"),
            P("tensor", "dp"),
        ),
        out_specs=(P("tensor", "dp"), P("dp", "tensor"), P("dp", "tensor"), P("tensor", "dp")),
        check_vma=False,
    )
```

```python
import jax
import jax.numpy as jnp
from jax import lax
from jax.experimental import pallas as pl
from jax.experimental.pallas import tpu as pltpu
from jax.sharding import PartitionSpec as P

BLOCK = 128
MESH = pl.DeviceIdType.MESH
F32 = jnp.float32
BF16 = jnp.bfloat16


def hadamard():
    common = lax.broadcasted_iota(jnp.int32, (BLOCK, BLOCK), 0) & lax.broadcasted_iota(
        jnp.int32, (BLOCK, BLOCK), 1
    )
    for shift in (4, 2, 1):
        common = common ^ (common >> shift)
    return (1 - 2 * (common & 1)).astype(F32).astype(BF16)


def dot(left, right, left_dim, right_dim):
    return lax.dot_general(
        left, right, (((left_dim,), (right_dim,)), ((), ())), preferred_element_type=F32
    )


def kernel(
    grad_ref, rot_ref, scale_ref, gate_ref, up_ref, gw_ref, uw_ref, dw_ref,
    ig_ref, gwg_ref, uwg_ref, dwg_ref,
    grads, normed, ug, part, crp, crm, xr, hg, ab, hid, gu, igp, xc, es, erp, erm, eap, eam, eh,
    wgu, dwp, rot, scale, gate, up, load_sem, send_sem, recv_sem,
):
    d = lax.axis_index("dp")
    t = lax.axis_index("tensor")
    xl, y = d // 8, d % 8
    z, h, c = t // 4, (t // 2) % 2, t % 2

    def at_y(k):
        return (y + (k + 8)) % 8

    def at_z(k):
        return (z + (k + 8)) % 8

    def y_to(k):
        return {"dp": xl * 8 + at_y(k)}

    def z_to(k, column=h):
        return {"tensor": at_z(k) * 4 + column * 2 + c}

    x_mate = {"dp": (1 - xl) * 8 + y}
    h_mate = z_to(0, 1 - h)
    c_mate = {"tensor": z * 4 + h * 2 + (1 - c)}

    barrier = pltpu.get_barrier_semaphore()
    partners = [z_to(1), z_to(-1), z_to(1, 1 - h), z_to(-1, 1 - h), h_mate, c_mate]
    partners += [y_to(1), y_to(-1), x_mate, z_to(2), z_to(-2), z_to(2, 1 - h), z_to(-2, 1 - h)]
    for other in partners:
        pl.semaphore_signal(barrier, inc=1, device_id=other, device_id_type=MESH)

    def rows(half):
        return pl.ds(pl.multiple_of(half * 48, 16), 48)

    loads = []

    def load(src, dst):
        copy = pltpu.make_async_copy(src, dst, load_sem.at[len(loads)])
        copy.start()
        loads.append(copy)
        return copy

    own_piece = grads.at[2 * z + c, rows(h)]
    got_grad = load(grad_ref, own_piece)
    got_gate = [load(gate_ref, gate), load(up_ref, up)]
    got_rot = [load(rot_ref, rot), load(scale_ref, scale)]
    got_dw = load(dw_ref, dwp.at[0:448])
    got_w = [
        load(gw_ref.at[0:384], wgu.at[0:384]),
        load(uw_ref.at[0:384], wgu.at[384:768]),
        load(gw_ref.at[384:448], wgu.at[768:832]),
        load(uw_ref.at[384:448], wgu.at[832:896]),
    ]

    started = []

    def send(src, dst, to):
        index = len(started)
        copy = pltpu.make_async_remote_copy(
            src_ref=src,
            dst_ref=dst,
            send_sem=send_sem.at[index],
            recv_sem=recv_sem.at[index],
            device_id=to,
            device_id_type=MESH,
        )
        copy.start()
        started.append(copy)
        return copy

    low = lax.broadcasted_iota(jnp.int32, (48, 128), 1) < 64
    low96 = lax.broadcasted_iota(jnp.int32, (96, 128), 1) < 64

    def swap(value):
        return pltpu.roll(value, 64, 1)

    dwp[448:512, :] = jnp.zeros((64, 512), BF16)
    got_grad.wait()

    pl.semaphore_wait(barrier, len(partners))

    a_core = {}
    a_got = {}
    for k in (2, -2):
        for column in (0, 1):
            a_got[(k, column)] = send(own_piece, own_piece, z_to(k, h if column == 0 else 1 - h))
    a_x = send(own_piece, own_piece, h_mate)
    for k in (1, -1):
        for column in (0, 1):
            a_got[(k, column)] = send(own_piece, own_piece, z_to(k, h if column == 0 else 1 - h))

    for copy in got_gate:
        copy.wait()
    ug[d, :, 0:384] = gate[:, 0:384]
    ug[d, :, 384:768] = up[:, 0:384]
    ug[d, :, 768:896] = jnp.concatenate([gate[:, 384:448], up[:, 384:448]], axis=1)
    b_x = []
    q = (slice(0, 48), slice(48, 96))
    b_got = {}
    for half in (0, 1):
        for way in (1, -1):
            piece = ug.at[d, q[half if way == 1 else 1 - half]]
            b_got[(way, half if way == 1 else 1 - half)] = send(piece, piece, y_to(way))

    for copy in got_rot:
        copy.wait()
    table = hadamard()
    eye = lax.broadcasted_iota(jnp.int32, (48, 48), 0) == lax.broadcasted_iota(
        jnp.int32, (48, 48), 1
    )
    for b in range(4):
        cols = slice(128 * b, 128 * b + 128)
        mixed = dot(rot[:, cols], table, 1, 0)
        row = jnp.broadcast_to(scale[b : b + 1, :], (48, 48))
        column = jnp.sum(jnp.where(eye, row, 0.0), axis=1, keepdims=True)
        normed[2 * z + c, rows(h), cols] = (mixed * (column * BLOCK ** (-0.5))).astype(BF16)
    own_normed = normed.at[2 * z + c, rows(h)]
    n_x = send(own_normed, own_normed, h_mate)
    got_dw.wait()

    def a_share(k):
        block = grads.at[2 * at_z(k) + c]
        a_core[k] = send(block, block, c_mate)

    for way in (1, -1):
        for column in (0, 1):
            a_got[(2 * way, column)].wait_recv()
        block = grads.at[2 * at_z(-2 * way) + c]
        a_got[(3 * way, 0)] = send(block, block, z_to(way))
        piece = block.at[0:48] if way == 1 else block.at[48:96]
        a_got[(4 * way, 0)] = send(piece, piece, z_to(2 * way))
    a_x.wait_recv()
    a_share(0)
    for way in (1, -1):
        for column in (0, 1):
            a_got[(way, column)].wait_recv()
        a_share(-way)
    for way in (1, -1):
        a_share(-2 * way)

    def b_step(k):
        for first in (True, False):
            for way in (1, -1):
                half = 0 if (way == 1) == first else 1
                if k == 4 and not first:
                    continue
                b_got[(way, half)].wait_recv()
                piece = ug.at[xl * 8 + at_y(-way * k), q[half]]
                if k < 3 or (k == 3 and first):
                    b_got[(way, half)] = send(piece, piece, y_to(way))
        for way in (1, -1) if k < 4 else ():
            block = ug.at[xl * 8 + at_y(-way * k)]
            b_x.append(send(block, block, x_mate))

    def partial(k):
        a_core[k].wait_recv()
        j = at_z(k)
        value = dot(grads[pl.ds(2 * j, 2)].reshape(192, 512), dwp[...], 1, 1)
        first, second = value[0:96], value[96:192]
        part[j, :, 0:384] = first[:, 0:384].astype(BF16)
        part[j, :, 384:768] = second[:, 0:384].astype(BF16)
        tail = jnp.where(low96, first[:, 384:512], swap(second[:, 384:512]))
        part[j, :, 768:896] = tail.astype(BF16)

    def factors(e):
        j, hh = e // 2, e % 2
        for cc in (0, 1):
            tile = ug[e, 48 * cc : 48 * cc + 48, :].astype(F32)
            tail = tile[:, 768:896]
            other = swap(tail)

            def parts(g, u):
                s = 1.0 / (1.0 + jnp.exp(-g))
                act = g * s
                return (u * s) * (1.0 + g * (1.0 - s)), act, act * u

            first, second, third = parts(tile[:, 0:384], tile[:, 384:768])
            ab[2 * j + cc, rows(hh), 0:384] = first
            ab[2 * j + cc, rows(hh), 384:768] = second
            hid[2 * j + cc, rows(hh), 0:384] = third.astype(BF16)
            first, second, third = parts(jnp.where(low, tail, other), jnp.where(low, other, tail))
            ab[2 * j + cc, rows(hh), 768:896] = jnp.where(low, first, second)
            hid[2 * j + cc, rows(hh), 384:512] = third.astype(BF16)

    b_x.append(send(ug.at[d], ug.at[d], x_mate))
    b_step(1)
    for k in (0, 1, -1):
        partial(k)
    for k in (2, -2):
        partial(k)
    for way in (1, -1):
        a_got[(3 * way, 0)].wait_recv()
        a_share(-3 * way)
    for way in (1, -1):
        a_got[(4 * way, 0)].wait_recv()
    a_share(4)
    b_step(2)
    for k in (3, -3, 4):
        partial(k)

    boxes = {1: crp, -1: crm}
    spans_c = {
        1: (slice(0, 32), slice(32, 48), slice(48, 96)),
        -1: (slice(64, 96), slice(48, 64), slice(0, 48)),
    }
    in_half = {0: ((1, 0), (1, 1), (-1, 2)), 1: ((-1, 0), (-1, 1), (1, 2))}
    c_got = {}

    def c_send(way, p, hop):
        span = spans_c[way][p]
        c_got[(way, p, hop)] = send(
            part.at[at_y(way * (4 - hop)), span], boxes[way].at[hop, span], y_to(way)
        )

    def c_add(way, p, hop):
        c_got[(way, p, hop - 1)].wait_recv()
        j = at_y(way * (4 - hop))
        span = spans_c[way][p]
        came = boxes[way][hop - 1, span, :].astype(F32)
        part[j, span, :] = (part[j, span, :].astype(F32) + came).astype(BF16)

    for p in (0, 1):
        for way in (1, -1):
            c_send(way, p, 0)
    for way in (1, -1):
        c_send(way, 2, 1)

    n_x.wait_recv()
    n_block = normed.at[2 * z + c]
    n_got = {1: send(n_block, n_block, z_to(1)), -1: send(n_block, n_block, z_to(-1))}
    n_core = [send(n_block, n_block, c_mate)]

    def n_step(k):
        after = {}
        for way in (1, -1):
            if way not in n_got:
                continue
            n_got[way].wait_recv()
            block = normed.at[2 * at_z(-way * k) + c]
            half = block.at[0:48] if way == 1 else block.at[48:96]
            if k == 4:
                block = half
            if k < 3:
                after[way] = send(block, block, z_to(way))
            elif k == 3:
                after[way] = send(half, half, z_to(way))
            n_core.append(send(block, block, c_mate))
        n_got.clear()
        n_got.update(after)

    for hop in (1, 2, 3):
        for p in (0, 1):
            for way in (1, -1):
                c_add(way, p, hop)
                c_send(way, p, hop)
        if hop < 3:
            for way in (1, -1):
                c_add(way, 2, hop + 1)
                c_send(way, 2, hop + 1)
        if hop == 1:
            b_step(3)
            n_step(1)
            for k in range(0, 3):
                factors(xl * 8 + at_y(k))
        elif hop == 2:
            n_step(2)
            for k in (3, 5):
                factors(xl * 8 + at_y(k))
    x_got = {}
    for half in (1, 0):
        for way, p in in_half[half]:
            c_got[(way, p, 3)].wait_recv()
        total = part[y, q[half], :].astype(F32) + crp[3, q[half], :].astype(F32)
        part[y, q[half], :] = (total + crm[3, q[half], :].astype(F32)).astype(BF16)
        x_got[half] = send(part.at[y, q[half]], xr.at[q[half]], x_mate)
    b_step(4)
    block = ug.at[xl * 8 + at_y(4)]
    b_x.append(send(block, block, x_mate))
    d_got = {}
    for half in (1, 0):
        x_got[half].wait_recv()
        total = part[y, q[half], :].astype(F32) + xr[q[half], :].astype(F32)
        hg[y, q[half], :] = total.astype(BF16)
        for way, p in in_half[half]:
            piece = hg.at[y, spans_c[way][p]]
            d_got[(way, p)] = send(piece, piece, y_to(way))

    n_step(3)
    for k in (4, 6, 7):
        factors(xl * 8 + at_y(k))
    def other_factors(k, carry):
        factors((1 - xl) * 8 + (y + k) % 8)
        return carry

    e_core = {}

    def back(k):
        j = at_y(k)
        block = hg[j].astype(F32)
        tail = block[:, 768:896]
        other = swap(tail)
        for cc in (0, 1):
            main = block[:, 384 * cc : 384 * cc + 384]
            both = jnp.where(low96, tail, other) if cc == 0 else jnp.where(low96, other, tail)
            gu[2 * j + cc, :, 0:384] = (ab[2 * j + cc, :, 0:384] * main).astype(BF16)
            gu[2 * j + cc, :, 384:768] = (ab[2 * j + cc, :, 384:768] * main).astype(BF16)
            gu[2 * j + cc, :, 768:896] = (ab[2 * j + cc, :, 768:896] * both).astype(BF16)
        value = dot(gu[pl.ds(2 * j, 2)].reshape(192, 896), wgu[...], 1, 0).astype(BF16)
        igp[2 * j] = value[0:96]
        igp[2 * j + 1] = value[96:192]
        e_core[k] = send(igp.at[2 * j + 1 - c], xc.at[j], c_mate)

    def d_step(k):
        for p in (0, 1, 2):
            for way in (1, -1):
                if k == 4 and p == 2:
                    continue
                d_got[(way, p)].wait_recv()
                piece = hg.at[at_y(-way * k), spans_c[way][p]]
                if k < 3 or (k == 3 and p < 2):
                    d_got[(way, p)] = send(piece, piece, y_to(way))

    d_step(1)
    for copy in b_x[0:5]:
        copy.wait_recv()
    lax.fori_loop(0, 3, other_factors, 0)
    lax.fori_loop(6, 8, other_factors, 0)
    d_step(2)
    for copy in b_x[5:8]:
        copy.wait_recv()
    lax.fori_loop(3, 6, other_factors, 0)
    for copy in got_w:
        copy.wait()
    d_step(3)
    early = len(started) - 40
    for copy in started[:early]:
        copy.wait_send()
    for k in (0, 1, -1, 2, -2):
        back(k)
    n_step(4)
    back(3)
    back(-3)
    d_step(4)
    back(4)

    for copy in e_core.values():
        copy.wait_recv()

    def mine(j, span):
        return igp[2 * j + c, span, :].astype(F32) + xc[j, span, :].astype(F32)

    def weight_grads(m):
        cols = slice(128 * m, 128 * m + 128)
        value = dot(gu[:, :, cols].reshape(1536, 128), normed[...].reshape(1536, 512), 0, 0)
        value = value.astype(BF16)
        if m < 3:
            gwg_ref[cols, :] = value
        elif m < 6:
            uwg_ref[128 * (m - 3) : 128 * (m - 2), :] = value
        else:
            gwg_ref[384:448, :] = value[0:64]
            uwg_ref[384:448, :] = value[64:128]

    spans = (rows(h), rows(1 - h))
    boxes_e = {1: erp, -1: erm}
    e_far = {}
    e_got = {}
    e_near = {}
    def down_grads(m):
        cols = slice(256 * m, 256 * m + 256)
        value = dot(hid[:, :, cols].reshape(1536, 256), grads[...].reshape(1536, 512), 0, 0)
        size = 256 if m == 0 else 192
        dwg_ref[256 * m : 256 * m + size, :] = value[0:size].astype(BF16)

    j4 = at_z(4)
    es[z, spans[1], :] = mine(z, spans[1]).astype(BF16)
    for way, column, box in ((1, 1, eap), (-1, 0, eam)):
        es[j4, spans[column], :] = mine(j4, spans[column]).astype(BF16)
        e_far[way] = send(es.at[j4, spans[column]], box, z_to(2 * way))
    for hop in (0, 1):
        for column in (1, 0):
            for way in (1, -1):
                j = at_z(way * (3 - hop))
                span = spans[column]
                value = mine(j, span)
                if hop > 0:
                    e_got[(way, column)].wait_recv()
                    value = value + boxes_e[way][0, span, :].astype(F32)
                if hop == 1 and way == (1 if column == 1 else -1):
                    e_far[way].wait_recv()
                    value = value + (eap if way == 1 else eam)[...].astype(F32)
                es[j, span, :] = value.astype(BF16)
                if hop == 0:
                    box = boxes_e[way].at[0, span]
                    e_got[(way, column)] = send(es.at[j, span], box, z_to(way))
                elif column == 1:
                    box = eh.at[3 if way == 1 else 4]
                    e_got[(way, 1)] = send(es.at[j, span], box, z_to(2 * way, 1 - h))
                else:
                    box = boxes_e[way].at[2, span]
                    e_got[(way, 0)] = send(es.at[j, span], box, z_to(2 * way))
        if hop == 0:
            for column in (1, 0):
                for way in (1, -1):
                    j = at_z(way)
                    span = spans[column]
                    es[j, span, :] = mine(j, span).astype(BF16)
                    if column == 1:
                        box = eh.at[0 if way == 1 else 1]
                        e_near[(way, 1)] = send(es.at[j, span], box, z_to(way, 1 - h))
                    else:
                        box = boxes_e[way].at[1, span]
                        e_near[(way, 0)] = send(es.at[j, span], box, z_to(way))
        if hop == 0:
            e_mate = send(es.at[z, spans[1]], eh.at[2], h_mate)
            down_grads(0)
            for copy in n_core:
                copy.wait_recv()
            for m in range(0, 3):
                weight_grads(m)
        else:
            for m in range(3, 7):
                weight_grads(m)
    down_grads(1)

    total = mine(z, spans[0])
    for way in (1, -1):
        e_near[(way, 0)].wait_recv()
        e_got[(way, 0)].wait_recv()
        total = total + boxes_e[way][1, spans[0], :].astype(F32)
        total = total + boxes_e[way][2, spans[0], :].astype(F32)
    e_mate.wait_recv()
    total = total + eh[2].astype(F32)
    for copy in started[early:]:
        copy.wait_send()
    for way in (1, -1):
        e_near[(way, 1)].wait_recv()
        e_got[(way, 1)].wait_recv()
    for i in (0, 1, 3, 4):
        total = total + eh[i].astype(F32)
    ig_ref[...] = total.astype(BF16)


COPIES = 250


def shards(grad_out, rot, scale, gate, up, gate_weight, up_weight, down_weight):
    vmem = pl.BlockSpec(memory_space=pltpu.VMEM)
    shapes = [
        ((16, 96, 512), BF16),
        ((16, 96, 512), BF16),
        ((16, 96, 896), BF16),
        ((8, 96, 896), BF16),
        ((4, 96, 896), BF16),
        ((4, 96, 896), BF16),
        ((96, 896), BF16),
        ((8, 96, 896), BF16),
        ((16, 96, 896), F32),
        ((16, 96, 512), BF16),
        ((16, 96, 896), BF16),
        ((16, 96, 512), BF16),
        ((8, 96, 512), BF16),
        ((8, 96, 512), BF16),
        ((3, 96, 512), BF16),
        ((3, 96, 512), BF16),
        ((48, 512), BF16),
        ((48, 512), BF16),
        ((5, 48, 512), BF16),
        ((896, 512), BF16),
        ((512, 512), BF16),
        ((48, 512), BF16),
        ((4, 48), F32),
        ((96, 448), BF16),
        ((96, 448), BF16),
    ]
    operands = (grad_out, rot, scale.T, gate, up, gate_weight.T, up_weight.T, down_weight)
    operands = [pltpu.with_memory_space_constraint(each, pltpu.HBM) for each in operands]
    ig, gwg, uwg, dwg = pl.pallas_call(
        kernel,
        out_shape=(
            pltpu.VMEM((48, 512), BF16),
            pltpu.VMEM((448, 512), BF16),
            pltpu.VMEM((448, 512), BF16),
            pltpu.VMEM((448, 512), BF16),
        ),
        in_specs=[pl.BlockSpec(memory_space=pl.ANY)] * 8,
        out_specs=(vmem,) * 4,
        scratch_shapes=[pltpu.VMEM(shape, kind) for shape, kind in shapes]
        + [
            pltpu.SemaphoreType.DMA((16,)),
            pltpu.SemaphoreType.DMA((COPIES,)),
            pltpu.SemaphoreType.DMA((COPIES,)),
        ],
        compiler_params=pltpu.CompilerParams(
            collective_id=0, has_side_effects=True, vmem_limit_bytes=48 * 1024 * 1024
        ),
    )(*operands)
    return ig, gwg.T, uwg.T, dwg


def solution(mesh):
    return jax.shard_map(
        shards,
        mesh=mesh,
        in_specs=(
            P("tensor", "dp"),
            P("tensor", "dp"),
            P("tensor", "dp"),
            P("dp", "tensor"),
            P("dp", "tensor"),
            P("dp", "tensor"),
            P("dp", "tensor"),
            P("tensor", "dp"),
        ),
        out_specs=(P("tensor", "dp"), P("dp", "tensor"), P("dp", "tensor"), P("tensor", "dp")),
        check_vma=False,
    )
```
